32 devices in a mesh: tm: 4 (over y, x), space: 8 (over z, core).
Axes of the slice: x: 2, y: 2, z: 4, core: 2. Of those that a mesh axis runs over, the one named last changes fastest.
Arguments:
- material_ids: int32 [128, 2048], P('space'), may hold values from 0 to 7
- conductivity_table: float32 [8], replicated, may hold values from 0.1 to 10
- c_points: float32 [4, 128, 2048], P('tm', 'space'), may hold values from -6 to 6
Outputs:
- f_points: float32 [4, 128, 2048], P('tm', 'space')
- next_c: float32 [4, 128, 2048], P('tm', 'space')
The draws below stay inside these ranges and needn't reach their ends.
All inputs are finite; a program needn't handle non-finite values.
Results may differ from the reference program's by a relative error of at most 0.00022.
Values sent between devices are 32-bit elements; how exact they have to be, the bound alone decides.
A program may use at most 64 MiB of HBM per device.

```python
import math
import jax
import jax.numpy as jnp
from jax import lax

NX = 2048
LEVELS = 5
PRE_SWEEPS = 2
POST_SWEEPS = 2
COARSE_SWEEPS = 16
MATS = 8
TGROUPS = 4
NY = 128


def draw_c_points(key, part):
    shape = (TGROUPS, NY, NX)
    noise_key = jax.random.fold_in(key, 11)
    phase_key = jax.random.fold_in(key, 12)
    phases = jax.random.uniform(phase_key, (TGROUPS, 2), jnp.float32, 0.0, 2.0 * math.pi)
    row_pos = (jnp.arange(NY).astype(jnp.float32) + 0.5)[None, :, None]
    col_pos = (jnp.arange(NX).astype(jnp.float32) + 0.5)[None, None, :]
    row_phase = phases[:, 0][:, None, None]
    col_phase = phases[:, 1][:, None, None]
    rough = 0.5 * jax.random.truncated_normal(noise_key, -3.0, 3.0, shape, jnp.float32)
    wave = jnp.sin(2.0 * math.pi * row_pos / 256.0 + row_phase) * jnp.sin(2.0 * math.pi * col_pos / 256.0 + col_phase)
    smooth = 4.5 * wave
    return rough + smooth


def place_ends(result, own_key, least, largest):
    index_at = [jax.random.randint(jax.random.fold_in(own_key, axis), (), 0, length) for axis, length in enumerate(result.shape)]
    widest = result.shape.index(max(result.shape))
    next_to = index_at[:widest] + [(index_at[widest] + 1) % result.shape[widest]] + index_at[widest + 1:]
    return result.at[tuple(index_at)].set(least).at[tuple(next_to)].set(largest)


def setup_inputs(seed: int = 0) -> dict:
    key_list = jax.random.split(jax.random.key(seed), 4)
    return {
        "material_ids": place_ends(jax.random.randint(key_list[0], (NY, NX), 0, MATS), jax.random.fold_in(key_list[0], 1), 0, MATS - 1).astype(jnp.int32),
        "conductivity_table": jnp.clip(jnp.exp(jax.random.uniform(key_list[1], (MATS,), jnp.float32, math.log(0.1), math.log(10.0))), 0.1, 10.0),
        "c_points": draw_c_points(jax.random.fold_in(key_list[3], 71), 0),
    }


DAMPING = 0.8
DIFFUSION = 1024.0


def lookup(material_ids, conductivity_table):
    conduct = jnp.zeros(material_ids.shape, jnp.float32)
    for material in range(MATS):
        conduct = conduct + jnp.where(material_ids == material, conductivity_table[material], jnp.float32(0.0))
    return conduct


def coarsen(values):
    row_count, col_count = values.shape
    blocks = values.reshape(row_count // 2, 2, col_count // 2, 2)
    return 0.25 * ((blocks[:, 0, :, 0] + blocks[:, 1, :, 0]) + (blocks[:, 0, :, 1] + blocks[:, 1, :, 1]))


def prolong(values):
    return jnp.repeat(jnp.repeat(values, 2, axis=0), 2, axis=1)


def coefficients(padded_conduct, face_scale):
    center = padded_conduct[1:-1, 1:-1]
    north_face = face_scale * 0.5 * (center + padded_conduct[:-2, 1:-1])
    south_face = face_scale * 0.5 * (center + padded_conduct[2:, 1:-1])
    west_face = face_scale * 0.5 * (center + padded_conduct[1:-1, :-2])
    east_face = face_scale * 0.5 * (center + padded_conduct[1:-1, 2:])
    diagonal = 1.0 + ((north_face + south_face) + (west_face + east_face))
    return (north_face, south_face, west_face, east_face, diagonal)


def operate(padded, coefs):
    north_face, south_face, west_face, east_face, diagonal = coefs
    center = padded[1:-1, 1:-1]
    beside_all = (north_face * padded[:-2, 1:-1] + south_face * padded[2:, 1:-1]) + (west_face * padded[1:-1, :-2] + east_face * padded[1:-1, 2:])
    return diagonal * center - beside_all


def sweeps(current, forcing, coefs, count):
    for sweep_no in range(count):
        current = current + DAMPING * ((forcing - operate(jnp.pad(current, 1), coefs)) / coefs[4])
    return current


def vcycle(depth_level, current, forcing, all_coefs):
    coefs = all_coefs[depth_level]
    if depth_level == LEVELS - 1:
        return sweeps(current, forcing, coefs, COARSE_SWEEPS)
    current = sweeps(current, forcing, coefs, PRE_SWEEPS)
    residue = forcing - operate(jnp.pad(current, 1), coefs)
    coarse_rhs = coarsen(residue)
    correct = vcycle(depth_level + 1, jnp.zeros_like(coarse_rhs), coarse_rhs, all_coefs)
    current = current + prolong(correct)
    return sweeps(current, forcing, coefs, POST_SWEEPS)


def reference(material_ids, conductivity_table, c_points):
    conduct = lookup(material_ids, conductivity_table)
    all_coefs = []
    for depth_level in range(LEVELS):
        all_coefs.append(coefficients(jnp.pad(conduct, 1), DIFFUSION / (4.0 ** depth_level)))
        if depth_level + 1 < LEVELS:
            conduct = coarsen(conduct)

    def propagate(start_field):
        first_step = vcycle(0, start_field, start_field, all_coefs)
        second_step = vcycle(0, first_step, first_step, all_coefs)
        return first_step, second_step

    f_points, end_fields = lax.map(propagate, c_points)
    next_c = jnp.concatenate([c_points[:1], end_fields[:-1]], axis=0)
    return f_points, next_c
```

```python
import functools

import jax
import jax.numpy as jnp
from jax import lax
from jax.experimental import pallas as pl
from jax.experimental.pallas import tpu as pltpu
from jax.sharding import PartitionSpec as P

MESH = pl.DeviceIdType.MESH
MATS = 8
COARSE_SWEEPS = 16
DIFFUSION = 1024.0
HALO = 12
H1 = HALO // 2
PAD = 2


def rows_loop(lo, hi, size, body):
    count = hi - lo
    full = count // size
    if full == 1:
        body(lo, size)
    elif full > 1:

        def step(i, carry):
            body(lo + i * size, size)
            return carry

        lax.fori_loop(0, full, step, 0)
    if count % size:
        body(lo + full * size, count % size)


def iota(shape, dim):
    return lax.broadcasted_iota(jnp.int32, shape, dim)


def roll(x, by, axis):
    return pltpu.roll(x, by, axis)


def from_west(x, d):
    r = roll(x, d, 2)
    return jnp.where(iota(x.shape, 2) < d, roll(r, 1, 1), r)


def from_east(x, d):
    r = roll(x, 128 - d, 2)
    return jnp.where(iota(x.shape, 2) >= 128 - d, roll(r, 7, 1), r)


def first_col(shape, d):
    return (iota(shape, 1) == 0) & (iota(shape, 2) < d)


def last_col(shape, d):
    return (iota(shape, 1) == 7) & (iota(shape, 2) >= 128 - d)


def partner(x, d):
    return jnp.where((iota(x.shape, 2) & d) == 0, roll(x, 128 - d, 2), roll(x, d, 2))


def pair_rows(x):
    x = x.reshape((x.shape[0] // 2, 2) + x.shape[1:])
    return x[:, 0], x[:, 1]


def restrict(x, d):
    a, b = pair_rows(x)
    t = a + b
    return 0.25 * (t + partner(t, d))


def split3(x):
    hi = x.astype(jnp.bfloat16)
    rest = x - hi.astype(jnp.float32)
    mid = rest.astype(jnp.bfloat16)
    lo = (rest - mid.astype(jnp.float32)).astype(jnp.bfloat16)
    return hi, mid, lo


def dot(a, b):
    return jnp.dot(a, b, preferred_element_type=jnp.float32)


class Level:
    def __init__(self, refs, d, scale, size):
        self.cond, self.fv, self.w, self.e, self.diag, self.om, self.g, self.b, self.c = refs
        self.d, self.scale, self.size = d, scale, size

    def setup(self, lo, hi, first_row, last_row, base):
        d, half = self.d, self.scale * 0.5

        def body(r, c):
            cond = self.cond
            here = cond[pl.ds(r, c)]
            shape = here.shape
            n = half * (here + cond[pl.ds(r - 1, c)])
            s = half * (here + cond[pl.ds(r + 1, c)])
            out_w, out_e = first_col(shape, d), last_col(shape, d)
            w = half * (here + jnp.where(out_w, 0.0, from_west(here, d)))
            e = half * (here + jnp.where(out_e, 0.0, from_east(here, d)))
            diag = 1.0 + ((n + s) + (w + e))
            row = iota(shape, 0) + (r + base)
            self.fv[pl.ds(r, c)] = jnp.where((row > first_row) & (row <= last_row), n, 0.0)
            self.w[pl.ds(r, c)] = jnp.where(out_w, 0.0, w)
            self.e[pl.ds(r, c)] = jnp.where(out_e, 0.0, e)
            self.diag[pl.ds(r, c)] = diag
            self.om[pl.ds(r, c)] = 0.8 / diag

        rows_loop(lo, hi, self.size, body)

    def beside(self, v, r, c):
        here = v[pl.ds(r, c)]
        nb = (
            self.fv[pl.ds(r, c)] * v[pl.ds(r - 1, c)]
            + self.fv[pl.ds(r + 1, c)] * v[pl.ds(r + 1, c)]
        ) + (
            self.w[pl.ds(r, c)] * from_west(here, self.d)
            + self.e[pl.ds(r, c)] * from_east(here, self.d)
        )
        return here, nb

    def start(self, lo, hi, dst):
        def body(r, c):
            dst[pl.ds(r, c)] = self.om[pl.ds(r, c)] * self.g[pl.ds(r, c)]

        rows_loop(lo, hi, self.size, body)

    def sweep(self, lo, hi, src, dst):
        def body(r, c):
            here, nb = self.beside(src, r, c)
            dst[pl.ds(r, c)] = 0.2 * here + self.om[pl.ds(r, c)] * (self.g[pl.ds(r, c)] + nb)

        rows_loop(lo, hi, self.size, body)

    def residue(self, v, r, c):
        here, nb = self.beside(v, r, c)
        return self.g[pl.ds(r, c)] - (self.diag[pl.ds(r, c)] * here - nb)


def kernel(
    n, intervals, ny,
    ids_ref, table_ref, c_ref, f_ref, out_ref,
    turn, start_w, first_w, b0, c0, cond0, fv0, w0, e0, diag0, om0,
    cond1, fv1, w1, e1, diag1, om1, g1, b1, c1,
    cond2, fv2, w2, e2, diag2, om2, g2, b2, c2,
    cond3, fv3, w3, e3, diag3, om3, g3, b3, c3,
    cond4, fv4, w4, e4, diag4, om4, g4, b4, c4,
    gather_cond, gather_1, gather_2, end_nat,
    halo_send, halo_recv, gat_send, gat_recv, end_send, end_recv,
):
    me = lax.axis_index("space")
    mine_t = lax.axis_index("tm")
    R = c_ref.shape[1]
    top, bottom = HALO, HALO + R
    window = R + 2 * HALO

    barrier = pltpu.get_barrier_semaphore()
    for j in range(1, n):
        pl.semaphore_signal(barrier, 1, device_id={"space": lax.rem(me + j, n)}, device_id_type=MESH)

    for j in (1, intervals - 1):
        next_t = lax.rem(mine_t + j, intervals)
        pl.semaphore_signal(barrier, 1, device_id={"tm": next_t}, device_id_type=MESH)

    def halo_copies(ref, which):
        up = pltpu.make_async_remote_copy(
            src_ref=ref.at[pl.ds(top, HALO)],
            dst_ref=ref.at[pl.ds(bottom, HALO)],
            send_sem=halo_send.at[2 * which],
            recv_sem=halo_recv.at[2 * which],
            device_id={"space": lax.rem(me + n - 1, n)},
            device_id_type=MESH,
        )
        down = pltpu.make_async_remote_copy(
            src_ref=ref.at[pl.ds(bottom - HALO, HALO)],
            dst_ref=ref.at[pl.ds(0, HALO)],
            send_sem=halo_send.at[2 * which + 1],
            recv_sem=halo_recv.at[2 * which + 1],
            device_id={"space": lax.rem(me + 1, n)},
            device_id_type=MESH,
        )
        return up, down

    def halo_start(ref, which):
        up, down = halo_copies(ref, which)

        @pl.when(me > 0)
        def _():
            up.start()

        @pl.when(me < n - 1)
        def _():
            down.start()

    def halo_arrive(ref, which):
        up, down = halo_copies(ref, which)
        zero = jnp.zeros((HALO,) + ref.shape[1:], jnp.float32)

        @pl.when(me > 0)
        def _():
            down.wait_recv()

        @pl.when(me == 0)
        def _():
            ref[pl.ds(0, HALO)] = zero

        @pl.when(me < n - 1)
        def _():
            up.wait_recv()

        @pl.when(me == n - 1)
        def _():
            ref[pl.ds(bottom, HALO)] = zero

    def halo_sent(ref, which):
        up, down = halo_copies(ref, which)

        @pl.when(me > 0)
        def _():
            up.wait_send()

        @pl.when(me < n - 1)
        def _():
            down.wait_send()

    def gather_copy(ref, which, j, slot):
        return pltpu.make_async_remote_copy(
            src_ref=ref.at[slot],
            dst_ref=ref.at[slot],
            send_sem=gat_send.at[which * n + j],
            recv_sem=gat_recv.at[which * n + j],
            device_id={"space": lax.rem(me + j, n)},
            device_id_type=MESH,
        )

    def gather_start(ref, which):
        for j in range(1, n):
            gather_copy(ref, which, j, me).start()

    def gather_arrive(ref, which):
        for j in range(1, n):
            gather_copy(ref, which, j, lax.rem(me + n - j, n)).wait_recv()

    def gather_sent(ref, which):
        for j in range(1, n):
            gather_copy(ref, which, j, me).wait_send()

    row_i, col_i = iota((256, 256), 0), iota((256, 256), 1)
    into = jnp.where(col_i == (row_i & 1) * 128 + (row_i >> 1), 1.0, 0.0).astype(jnp.bfloat16)

    def put_turned(y):
        for k in range(2):
            turn[pl.ds(k * 8 * R, 8 * R), :] = y[:, k * 128 : (k + 1) * 128]

    def chunks(x):
        return jnp.concatenate([x[:, s * 256 : (s + 1) * 256] for s in range(8)], axis=0)

    put_turned(dot(chunks(ids_ref[...].astype(jnp.float32)).astype(jnp.bfloat16), into))
    for r in range(R):
        for k in range(2):
            kind = turn[pl.ds(k * 8 * R + r, 8, stride=R), :]
            value = jnp.zeros((8, 128), jnp.float32)
            for m in range(MATS):
                value = jnp.where(kind == float(m), table_ref[m], value)
            cond0[top + r, k] = value

    put_turned(sum(dot(part, into) for part in split3(chunks(c_ref[0]))))
    for r in range(R):
        for k in range(2):
            start_w[top + r, k] = turn[pl.ds(k * 8 * R + r, 8, stride=R), :]

    def natural(src, row0, store):
        for r in range(R):
            for k in range(2):
                turn[pl.ds(k * 8 * R + r, 8, stride=R), :] = src[row0 + r, k]
        back = jnp.where(row_i == (col_i & 1) * 128 + (col_i >> 1), 1.0, 0.0).astype(jnp.bfloat16)
        x = jnp.concatenate(
            [turn[pl.ds(0, 8 * R), :], turn[pl.ds(8 * R, 8 * R), :]], axis=1
        )
        y = sum(dot(part, back) for part in split3(x))
        for s in range(8):
            store(s, y[s * R : (s + 1) * R])

    pl.semaphore_wait(barrier, n + 1)

    halo_start(cond0, 0)
    halo_start(start_w, 1)

    scale = DIFFUSION
    L1 = Level((cond1, fv1, w1, e1, diag1, om1, g1, b1, c1), 1, scale / 4, 7)
    L2 = Level((cond2, fv2, w2, e2, diag2, om2, g2, b2, c2), 2, scale / 16, 8)
    L3 = Level((cond3, fv3, w3, e3, diag3, om3, g3, b3, c3), 4, scale / 64, 8)
    L4 = Level((cond4, fv4, w4, e4, diag4, om4, g4, b4, c4), 8, scale / 256, 8)
    ny2, ny3, ny4 = ny // 4, ny // 8, ny // 16

    def coarsen_cond(lo, hi):
        def body(j, c):
            x = cond0[pl.ds(2 * j, 2 * c)]
            a, b = pair_rows(x)
            t = a + b
            cond1[pl.ds(j, c)] = 0.25 * (t[:, 0] + t[:, 1])

        rows_loop(lo, hi, 4, body)

    coarsen_cond(H1, H1 + R // 2)
    gather_cond[me] = pack4(restrict(cond1[pl.ds(H1, R // 2)], 1))
    gather_start(gather_cond, 0)

    zero_pad = jnp.zeros((PAD, 8, 128), jnp.float32)
    for level, rows in ((L2, ny2), (L3, ny3), (L4, ny4)):
        for ref in (level.cond, level.b, level.c, level.fv):
            ref[pl.ds(0, PAD)] = zero_pad
            ref[pl.ds(PAD + rows, PAD)] = zero_pad

    gather_arrive(gather_cond, 0)
    unpack4(gather_cond, cond2)
    cond3[pl.ds(PAD, ny3)] = restrict(cond2[pl.ds(PAD, ny2)], 2)
    cond4[pl.ds(PAD, ny4)] = restrict(cond3[pl.ds(PAD, ny3)], 4)
    for level, rows in ((L2, ny2), (L3, ny3), (L4, ny4)):
        level.setup(PAD, PAD + rows, 0, rows - 1, -PAD)

    halo_arrive(cond0, 0)
    coarsen_cond(0, H1)
    coarsen_cond(H1 + R // 2, R // 2 + 2 * H1)
    base0 = me * R - HALO
    half0 = scale * 0.5

    def setup0(r, c):
        here0, here1 = cond0[pl.ds(r, c), 0], cond0[pl.ds(r, c), 1]
        shape = here0.shape
        out_w, out_e = first_col(shape, 1), last_col(shape, 1)
        mid = half0 * (here0 + here1)
        west = half0 * (here0 + jnp.where(out_w, 0.0, from_west(here1, 1)))
        east = half0 * (here1 + jnp.where(out_e, 0.0, from_east(here0, 1)))
        row = iota(shape, 0) + (r + base0)
        inside = (row > 0) & (row <= ny - 1)
        for k, here, we in ((0, here0, west + mid), (1, here1, mid + east)):
            north = half0 * (here + cond0[pl.ds(r - 1, c), k])
            south = half0 * (here + cond0[pl.ds(r + 1, c), k])
            diag = 1.0 + ((north + south) + we)
            fv0[pl.ds(r, c), k] = jnp.where(inside, north, 0.0)
            diag0[pl.ds(r, c), k] = diag
            om0[pl.ds(r, c), k] = 0.8 / diag
        w0[pl.ds(r, c), 0] = jnp.where(out_w, 0.0, west)
        w0[pl.ds(r, c), 1] = mid
        e0[pl.ds(r, c)] = jnp.where(out_e, 0.0, east)

    rows_loop(1, window - 1, 4, setup0)
    L1.setup(1, R // 2 + 2 * H1 - 1, 0, ny // 2 - 1, me * (R // 2) - H1)

    def beside0(v, r, c):
        v0, v1 = v[pl.ds(r, c), 0], v[pl.ds(r, c), 1]
        up, down = pl.ds(r - 1, c), pl.ds(r + 1, c)
        at = pl.ds(r, c)
        mid = w0[at, 1]
        nb0 = (fv0[at, 0] * v[up, 0] + fv0[down, 0] * v[down, 0]) + (
            w0[at, 0] * from_west(v1, 1) + mid * v1
        )
        nb1 = (fv0[at, 1] * v[up, 1] + fv0[down, 1] * v[down, 1]) + (
            mid * v0 + e0[at] * from_east(v0, 1)
        )
        return (v0, v1), (nb0, nb1)

    def sweep0(lo, hi, src, g, dst):
        def body(r, c):
            here, nb = beside0(src, r, c)
            at = pl.ds(r, c)
            for k in range(2):
                dst[at, k] = 0.2 * here[k] + om0[at, k] * (g[at, k] + nb[k])

        rows_loop(lo, hi, 6, body)

    def vcycle(g0, gathered, which, dst):
        sweep0(top - 10, bottom + 10, g0, g0, b0)
        sweep0(top - 9, bottom + 9, b0, g0, c0)

        def to_level_1(j, c):
            r, rows = 2 * j, 2 * c
            here, nb = beside0(c0, r, rows)
            at = pl.ds(r, rows)
            r0 = g0[at, 0] - (diag0[at, 0] * here[0] - nb[0])
            r1 = g0[at, 1] - (diag0[at, 1] * here[1] - nb[1])
            a, b = pair_rows(r0 + r1)
            g1[pl.ds(j, c)] = 0.25 * (a + b)

        own1, end1 = H1, H1 + R // 2
        rows_loop(own1 - 4, end1 + 4, 4, to_level_1)
        L1.start(own1 - 4, end1 + 4, b1)
        L1.sweep(own1 - 3, end1 + 3, b1, c1)
        gathered[me] = pack4(restrict(L1.residue(c1, own1, R // 2), 1))
        gather_start(gathered, which)
        gather_arrive(gathered, which)
        unpack4(gathered, g2)

        def down(level, rows, coarse):
            level.start(PAD, PAD + rows, level.b)
            level.sweep(PAD, PAD + rows, level.b, level.c)

            def body(j, c):
                coarse.g[pl.ds(PAD + j, c)] = restrict(
                    level.residue(level.c, PAD + 2 * j, 2 * c), level.d
                )

            rows_loop(0, rows // 2, 4, body)

        def up(level, rows, e_ref):
            def body(j, c):
                at = pl.ds(PAD + 2 * j, 2 * c)
                e = e_ref[pl.ds(PAD + j, c)]
                twice = jnp.stack([e, e], axis=1).reshape((2 * c, 8, 128))
                level.c[at] = level.c[at] + twice

            rows_loop(0, rows // 2, 4, body)
            level.sweep(PAD, PAD + rows, level.c, level.b)
            level.sweep(PAD, PAD + rows, level.b, level.c)

        down(L2, ny2, L3)
        down(L3, ny3, L4)
        L4.start(PAD, PAD + ny4, L4.b)
        L4.sweep(PAD, PAD + ny4, L4.b, L4.c)

        def twice_4(i, carry):
            L4.sweep(PAD, PAD + ny4, L4.c, L4.b)
            L4.sweep(PAD, PAD + ny4, L4.b, L4.c)
            return carry

        lax.fori_loop(0, (COARSE_SWEEPS - 2) // 2, twice_4, 0)
        up(L3, ny3, L4.c)
        up(L2, ny2, L3.c)

        first2 = PAD + me * (R // 4)
        for j in range(own1 - 3, end1 + 3):
            c1[j] = c1[j] + c2[first2 + (j - H1) // 2]
        L1.sweep(own1 - 2, end1 + 2, c1, b1)
        L1.sweep(own1 - 1, end1 + 1, b1, c1)

        def add_fine(j, c):
            at = pl.ds(2 * j, 2 * c)
            e = c1[pl.ds(j, c)]
            twice = jnp.stack([e, e], axis=1).reshape((2 * c, 8, 128))
            for k in range(2):
                c0[at, k] = c0[at, k] + twice

        rows_loop(own1 - 1, end1 + 1, 5, add_fine)
        sweep0(top - 1, bottom + 1, c0, g0, b0)
        sweep0(top, bottom, b0, g0, dst)

    halo_arrive(start_w, 1)
    vcycle(start_w, gather_1, 1, first_w)
    halo_start(first_w, 2)

    def store_f(s, y):
        f_ref[0, :, s * 256 : (s + 1) * 256] = y

    natural(first_w, top, store_f)
    halo_arrive(first_w, 2)
    vcycle(first_w, gather_2, 2, c0)

    def store_end(s, y):
        end_nat[:, s * 256 : (s + 1) * 256] = y

    natural(c0, top, store_end)
    to_next = pltpu.make_async_remote_copy(
        src_ref=end_nat,
        dst_ref=out_ref.at[0],
        send_sem=end_send,
        recv_sem=end_recv,
        device_id={"tm": lax.rem(mine_t + 1, intervals)},
        device_id_type=MESH,
    )

    @pl.when(mine_t < intervals - 1)
    def _():
        to_next.start()

    @pl.when(mine_t == 0)
    def _():
        out_ref[...] = c_ref[...]

    halo_sent(cond0, 0)
    halo_sent(start_w, 1)
    halo_sent(first_w, 2)
    gather_sent(gather_cond, 0)
    gather_sent(gather_1, 1)
    gather_sent(gather_2, 2)

    @pl.when(mine_t > 0)
    def _():
        to_next.wait_recv()

    @pl.when(mine_t < intervals - 1)
    def _():
        to_next.wait_send()


def pack4(x):
    a, b = pair_rows(x)
    return jnp.where((iota(a.shape, 2) & 1) == 0, a, b)


def unpack4(ref, dst):
    x = ref[...]
    x = x.reshape((x.shape[0] * x.shape[1],) + x.shape[2:])
    even = (iota(x.shape, 2) & 1) == 0
    a = jnp.where(even, x, roll(x, 1, 2))
    b = jnp.where(even, roll(x, 127, 2), x)
    rows = x.shape[0]
    dst[pl.ds(PAD, 2 * rows)] = jnp.stack([a, b], axis=1).reshape((2 * rows,) + x.shape[1:])


def solution(mesh):
    n, intervals = mesh.shape["space"], mesh.shape["tm"]

    def per_device(ids, table, c_points):
        _, R, nx = c_points.shape
        ny = R * n
        window = R + 2 * HALO
        f32 = jnp.float32

        def tiles(*lead):
            return pltpu.VMEM(lead + (8, 128), f32)

        scratch = [pltpu.VMEM((16 * R, 128), f32)]
        names = ["start_w", "first_w", "b0", "c0", "cond0", "fv0", "w0", "e0", "diag0", "om0"]
        for name in names:
            scratch.append(tiles(window) if name == "e0" else tiles(window, 2))
        scratch += [tiles(window // 2) for _ in range(9)]
        for level in (2, 3, 4):
            scratch += [tiles(ny // 2**level + 2 * PAD) for _ in range(9)]
        scratch += [tiles(n, R // 8) for _ in range(3)]
        scratch += [pltpu.VMEM((R, nx), f32)]
        scratch += [
            pltpu.SemaphoreType.DMA((6,)),
            pltpu.SemaphoreType.DMA((6,)),
            pltpu.SemaphoreType.DMA((3 * n,)),
            pltpu.SemaphoreType.DMA((3 * n,)),
            pltpu.SemaphoreType.DMA,
            pltpu.SemaphoreType.DMA,
        ]
        vmem = pl.BlockSpec(memory_space=pltpu.VMEM)
        return pl.pallas_call(
            functools.partial(kernel, n, intervals, ny),
            out_shape=[jax.ShapeDtypeStruct(c_points.shape, f32)] * 2,
            in_specs=[vmem, pl.BlockSpec(memory_space=pltpu.SMEM), vmem],
            out_specs=[vmem, vmem],
            scratch_shapes=scratch,
            compiler_params=pltpu.CompilerParams(
                collective_id=0, has_side_effects=True, vmem_limit_bytes=40 * 1024 * 1024
            ),
        )(ids, table, c_points)

    return jax.shard_map(
        per_device,
        mesh=mesh,
        in_specs=(P("space", None), P(), P("tm", "space", None)),
        out_specs=(P("tm", "space", None), P("tm", "space", None)),
        check_vma=False,
    )
```

```python
import functools

import jax
import jax.numpy as jnp
from jax import lax
from jax.experimental import pallas as pl
from jax.experimental.pallas import tpu as pltpu
from jax.sharding import PartitionSpec as P

MESH = pl.DeviceIdType.MESH
MATS = 8
COARSE_SWEEPS = 16
DIFFUSION = 1024.0
HALO = 12
H1 = HALO // 2
PAD = 2


def rows_loop(lo, hi, size, body):
    count = hi - lo
    full = count // size
    if full == 1:
        body(lo, size)
    elif full > 1:

        def step(i, carry):
            body(lo + i * size, size)
            return carry

        lax.fori_loop(0, full, step, 0)
    if count % size:
        body(lo + full * size, count % size)


def iota(shape, dim):
    return lax.broadcasted_iota(jnp.int32, shape, dim)


def roll(x, by, axis):
    return pltpu.roll(x, by, axis)


def from_west(x, d):
    r = roll(x, d, 2)
    return jnp.where(iota(x.shape, 2) < d, roll(r, 1, 1), r)


def from_east(x, d):
    r = roll(x, 128 - d, 2)
    return jnp.where(iota(x.shape, 2) >= 128 - d, roll(r, 7, 1), r)


def first_col(shape, d):
    return (iota(shape, 1) == 0) & (iota(shape, 2) < d)


def last_col(shape, d):
    return (iota(shape, 1) == 7) & (iota(shape, 2) >= 128 - d)


def partner(x, d):
    return jnp.where((iota(x.shape, 2) & d) == 0, roll(x, 128 - d, 2), roll(x, d, 2))


def pair_rows(x):
    x = x.reshape((x.shape[0] // 2, 2) + x.shape[1:])
    return x[:, 0], x[:, 1]


def restrict(x, d):
    a, b = pair_rows(x)
    t = a + b
    return 0.25 * (t + partner(t, d))


def split3(x):
    hi = x.astype(jnp.bfloat16)
    rest = x - hi.astype(jnp.float32)
    mid = rest.astype(jnp.bfloat16)
    lo = (rest - mid.astype(jnp.float32)).astype(jnp.bfloat16)
    return hi, mid, lo


def dot(a, b):
    return jnp.dot(a, b, preferred_element_type=jnp.float32)


class Level:
    def __init__(self, refs, d, scale, size):
        self.cond, self.fv, self.w, self.e, self.diag, self.om, self.g, self.b, self.c = refs
        self.d, self.scale, self.size = d, scale, size

    def setup(self, lo, hi, first_row, last_row, base):
        d, half = self.d, self.scale * 0.5

        def body(r, c):
            cond = self.cond
            here = cond[pl.ds(r, c)]
            shape = here.shape
            n = half * (here + cond[pl.ds(r - 1, c)])
            s = half * (here + cond[pl.ds(r + 1, c)])
            out_w, out_e = first_col(shape, d), last_col(shape, d)
            w = half * (here + jnp.where(out_w, 0.0, from_west(here, d)))
            e = half * (here + jnp.where(out_e, 0.0, from_east(here, d)))
            diag = 1.0 + ((n + s) + (w + e))
            row = iota(shape, 0) + (r + base)
            self.fv[pl.ds(r, c)] = jnp.where((row > first_row) & (row <= last_row), n, 0.0)
            self.w[pl.ds(r, c)] = jnp.where(out_w, 0.0, w)
            self.e[pl.ds(r, c)] = jnp.where(out_e, 0.0, e)
            self.diag[pl.ds(r, c)] = diag
            self.om[pl.ds(r, c)] = 0.8 / diag

        rows_loop(lo, hi, self.size, body)

    def beside(self, v, r, c):
        here = v[pl.ds(r, c)]
        nb = (
            self.fv[pl.ds(r, c)] * v[pl.ds(r - 1, c)]
            + self.fv[pl.ds(r + 1, c)] * v[pl.ds(r + 1, c)]
        ) + (
            self.w[pl.ds(r, c)] * from_west(here, self.d)
            + self.e[pl.ds(r, c)] * from_east(here, self.d)
        )
        return here, nb

    def start(self, lo, hi, dst):
        def body(r, c):
            dst[pl.ds(r, c)] = self.om[pl.ds(r, c)] * self.g[pl.ds(r, c)]

        rows_loop(lo, hi, self.size, body)

    def sweep(self, lo, hi, src, dst):
        def body(r, c):
            here, nb = self.beside(src, r, c)
            dst[pl.ds(r, c)] = 0.2 * here + self.om[pl.ds(r, c)] * (self.g[pl.ds(r, c)] + nb)

        rows_loop(lo, hi, self.size, body)

    def residue(self, v, r, c):
        here, nb = self.beside(v, r, c)
        return self.g[pl.ds(r, c)] - (self.diag[pl.ds(r, c)] * here - nb)


def kernel(
    n, intervals, ny,
    ids_hbm, table_ref, c_hbm, f_ref, out_ref,
    ids_ref, c_ref,
    turn, start_w, first_w, b0, c0, cond0, fv0, w0, e0, diag0, om0,
    cond1, fv1, w1, e1, diag1, om1, g1, b1, c1,
    cond2, fv2, w2, e2, diag2, om2, g2, b2, c2,
    cond3, fv3, w3, e3, diag3, om3, g3, b3, c3,
    cond4, fv4, w4, e4, diag4, om4, g4, b4, c4,
    gather_cond, gather_1, gather_2, end_nat,
    halo_send, halo_recv, gat_send, gat_recv, end_send, end_recv, in_sem,
):
    load_ids = pltpu.make_async_copy(ids_hbm, ids_ref, in_sem.at[0])
    load_c = pltpu.make_async_copy(c_hbm, c_ref, in_sem.at[1])
    load_ids.start()
    load_c.start()
    me = lax.axis_index("space")
    mine_t = lax.axis_index("tm")
    R = c_ref.shape[1]
    top, bottom = HALO, HALO + R
    window = R + 2 * HALO

    barrier = pltpu.get_barrier_semaphore()
    for j in range(1, n):
        pl.semaphore_signal(barrier, 1, device_id={"space": lax.rem(me + j, n)}, device_id_type=MESH)

    for j in (1, intervals - 1):
        next_t = lax.rem(mine_t + j, intervals)
        pl.semaphore_signal(barrier, 1, device_id={"tm": next_t}, device_id_type=MESH)

    def halo_copies(ref, which):
        up = pltpu.make_async_remote_copy(
            src_ref=ref.at[pl.ds(top, HALO)],
            dst_ref=ref.at[pl.ds(bottom, HALO)],
            send_sem=halo_send.at[2 * which],
            recv_sem=halo_recv.at[2 * which],
            device_id={"space": lax.rem(me + n - 1, n)},
            device_id_type=MESH,
        )
        down = pltpu.make_async_remote_copy(
            src_ref=ref.at[pl.ds(bottom - HALO, HALO)],
            dst_ref=ref.at[pl.ds(0, HALO)],
            send_sem=halo_send.at[2 * which + 1],
            recv_sem=halo_recv.at[2 * which + 1],
            device_id={"space": lax.rem(me + 1, n)},
            device_id_type=MESH,
        )
        return up, down

    def halo_start(ref, which):
        up, down = halo_copies(ref, which)

        @pl.when(me > 0)
        def _():
            up.start()

        @pl.when(me < n - 1)
        def _():
            down.start()

    def halo_arrive(ref, which):
        up, down = halo_copies(ref, which)
        zero = jnp.zeros((HALO,) + ref.shape[1:], jnp.float32)

        @pl.when(me > 0)
        def _():
            down.wait_recv()

        @pl.when(me == 0)
        def _():
            ref[pl.ds(0, HALO)] = zero

        @pl.when(me < n - 1)
        def _():
            up.wait_recv()

        @pl.when(me == n - 1)
        def _():
            ref[pl.ds(bottom, HALO)] = zero

    def halo_sent(ref, which):
        up, down = halo_copies(ref, which)

        @pl.when(me > 0)
        def _():
            up.wait_send()

        @pl.when(me < n - 1)
        def _():
            down.wait_send()

    def gather_copy(ref, which, j, slot):
        return pltpu.make_async_remote_copy(
            src_ref=ref.at[slot],
            dst_ref=ref.at[slot],
            send_sem=gat_send.at[which * n + j],
            recv_sem=gat_recv.at[which * n + j],
            device_id={"space": lax.rem(me + j, n)},
            device_id_type=MESH,
        )

    def gather_start(ref, which):
        for j in range(1, n):
            gather_copy(ref, which, j, me).start()

    def gather_arrive(ref, which):
        for j in range(1, n):
            gather_copy(ref, which, j, lax.rem(me + n - j, n)).wait_recv()

    def gather_sent(ref, which):
        for j in range(1, n):
            gather_copy(ref, which, j, me).wait_send()

    row_i, col_i = iota((256, 256), 0), iota((256, 256), 1)
    into = jnp.where(col_i == (row_i & 1) * 128 + (row_i >> 1), 1.0, 0.0).astype(jnp.bfloat16)

    def put_turned(y):
        for k in range(2):
            turn[pl.ds(k * 8 * R, 8 * R), :] = y[:, k * 128 : (k + 1) * 128]

    def chunks(x):
        return jnp.concatenate([x[:, s * 256 : (s + 1) * 256] for s in range(8)], axis=0)

    load_ids.wait()
    put_turned(dot(chunks(ids_ref[...].astype(jnp.float32)).astype(jnp.bfloat16), into))
    for r in range(R):
        for k in range(2):
            kind = turn[pl.ds(k * 8 * R + r, 8, stride=R), :]
            value = jnp.zeros((8, 128), jnp.float32)
            for m in range(MATS):
                value = jnp.where(kind == float(m), table_ref[m], value)
            cond0[top + r, k] = value

    def natural(src, row0, rows, base, store):
        for r in range(rows):
            for k in range(2):
                turn[pl.ds(base + k * 8 * rows + r, 8, stride=rows), :] = src[row0 + r, k]
        back = jnp.where(row_i == (col_i & 1) * 128 + (col_i >> 1), 1.0, 0.0).astype(jnp.bfloat16)
        x = jnp.concatenate(
            [turn[pl.ds(base, 8 * rows), :], turn[pl.ds(base + 8 * rows, 8 * rows), :]], axis=1
        )
        y = sum(dot(part, back) for part in split3(x))
        for s in range(8):
            store(s, y[s * rows : (s + 1) * rows])

    pl.semaphore_wait(barrier, n + 1)

    halo_start(cond0, 0)
    load_c.wait()
    put_turned(sum(dot(part, into) for part in split3(chunks(c_ref[0]))))
    for r in range(R):
        for k in range(2):
            start_w[top + r, k] = turn[pl.ds(k * 8 * R + r, 8, stride=R), :]
    halo_start(start_w, 1)

    scale = DIFFUSION
    L1 = Level((cond1, fv1, w1, e1, diag1, om1, g1, b1, c1), 1, scale / 4, 7)
    L2 = Level((cond2, fv2, w2, e2, diag2, om2, g2, b2, c2), 2, scale / 16, 16)
    L3 = Level((cond3, fv3, w3, e3, diag3, om3, g3, b3, c3), 4, scale / 64, 16)
    L4 = Level((cond4, fv4, w4, e4, diag4, om4, g4, b4, c4), 8, scale / 256, 8)
    ny2, ny3, ny4 = ny // 4, ny // 8, ny // 16

    def coarsen_cond(lo, hi):
        def body(j, c):
            x = cond0[pl.ds(2 * j, 2 * c)]
            a, b = pair_rows(x)
            t = a + b
            cond1[pl.ds(j, c)] = 0.25 * (t[:, 0] + t[:, 1])

        rows_loop(lo, hi, 4, body)

    coarsen_cond(H1, H1 + R // 2)
    gather_cond[me] = pack4(restrict(cond1[pl.ds(H1, R // 2)], 1))
    gather_start(gather_cond, 0)

    zero_pad = jnp.zeros((PAD, 8, 128), jnp.float32)
    for level, rows in ((L2, ny2), (L3, ny3), (L4, ny4)):
        for ref in (level.cond, level.b, level.c, level.fv):
            ref[pl.ds(0, PAD)] = zero_pad
            ref[pl.ds(PAD + rows, PAD)] = zero_pad

    halo_arrive(cond0, 0)
    coarsen_cond(0, H1)
    coarsen_cond(H1 + R // 2, R // 2 + 2 * H1)
    base0 = me * R - HALO
    half0 = scale * 0.5

    def setup0(r, c):
        here0, here1 = cond0[pl.ds(r, c), 0], cond0[pl.ds(r, c), 1]
        shape = here0.shape
        out_w, out_e = first_col(shape, 1), last_col(shape, 1)
        mid = half0 * (here0 + here1)
        west = half0 * (here0 + jnp.where(out_w, 0.0, from_west(here1, 1)))
        east = half0 * (here1 + jnp.where(out_e, 0.0, from_east(here0, 1)))
        row = iota(shape, 0) + (r + base0)
        inside = (row > 0) & (row <= ny - 1)
        for k, here, we in ((0, here0, west + mid), (1, here1, mid + east)):
            north = half0 * (here + cond0[pl.ds(r - 1, c), k])
            south = half0 * (here + cond0[pl.ds(r + 1, c), k])
            diag = 1.0 + ((north + south) + we)
            fv0[pl.ds(r, c), k] = jnp.where(inside, north, 0.0)
            diag0[pl.ds(r, c), k] = diag
            om0[pl.ds(r, c), k] = 0.8 / diag
        w0[pl.ds(r, c), 0] = jnp.where(out_w, 0.0, west)
        w0[pl.ds(r, c), 1] = mid
        e0[pl.ds(r, c)] = jnp.where(out_e, 0.0, east)

    rows_loop(1, window - 1, 4, setup0)
    L1.setup(1, R // 2 + 2 * H1 - 1, 0, ny // 2 - 1, me * (R // 2) - H1)

    def setup_low():
        gather_arrive(gather_cond, 0)
        unpack4(gather_cond, cond2)
        cond3[pl.ds(PAD, ny3)] = restrict(cond2[pl.ds(PAD, ny2)], 2)
        cond4[pl.ds(PAD, ny4)] = restrict(cond3[pl.ds(PAD, ny3)], 4)
        for level, rows in ((L2, ny2), (L3, ny3), (L4, ny4)):
            level.setup(PAD, PAD + rows, 0, rows - 1, -PAD)

    def beside0(v, r, c):
        v0, v1 = v[pl.ds(r, c), 0], v[pl.ds(r, c), 1]
        up, down = pl.ds(r - 1, c), pl.ds(r + 1, c)
        at = pl.ds(r, c)
        mid = w0[at, 1]
        nb0 = (fv0[at, 0] * v[up, 0] + fv0[down, 0] * v[down, 0]) + (
            w0[at, 0] * from_west(v1, 1) + mid * v1
        )
        nb1 = (fv0[at, 1] * v[up, 1] + fv0[down, 1] * v[down, 1]) + (
            mid * v0 + e0[at] * from_east(v0, 1)
        )
        return (v0, v1), (nb0, nb1)

    def sweep0(lo, hi, src, g, dst):
        def body(r, c):
            here, nb = beside0(src, r, c)
            at = pl.ds(r, c)
            for k in range(2):
                dst[at, k] = 0.2 * here[k] + om0[at, k] * (g[at, k] + nb[k])

        rows_loop(lo, hi, {14: 7, 8: 8, 16: 8}.get(hi - lo, 6), body)

    def vcycle(g0, gathered, which, dst):
        sweep0(top + 1, bottom - 1, g0, g0, b0)
        sweep0(top + 2, bottom - 2, b0, g0, c0)
        halo_arrive(g0, which)
        sweep0(top - 10, top + 1, g0, g0, b0)
        sweep0(bottom - 1, bottom + 10, g0, g0, b0)
        sweep0(top - 9, top + 2, b0, g0, c0)
        sweep0(bottom - 2, bottom + 9, b0, g0, c0)

        def to_level_1(j, c):
            r, rows = 2 * j, 2 * c
            here, nb = beside0(c0, r, rows)
            at = pl.ds(r, rows)
            r0 = g0[at, 0] - (diag0[at, 0] * here[0] - nb[0])
            r1 = g0[at, 1] - (diag0[at, 1] * here[1] - nb[1])
            a, b = pair_rows(r0 + r1)
            g1[pl.ds(j, c)] = 0.25 * (a + b)

        own1, end1 = H1, H1 + R // 2
        rows_loop(own1 - 4, end1 + 4, 4, to_level_1)
        L1.start(own1 - 4, end1 + 4, b1)
        L1.sweep(own1 - 3, end1 + 3, b1, c1)
        gathered[me] = pack4(restrict(L1.residue(c1, own1, R // 2), 1))
        gather_start(gathered, which)
        if which == 1:
            setup_low()
        gather_arrive(gathered, which)
        unpack4(gathered, g2)

        def down(level, rows, coarse):
            level.start(PAD, PAD + rows, level.b)
            level.sweep(PAD, PAD + rows, level.b, level.c)

            def body(j, c):
                coarse.g[pl.ds(PAD + j, c)] = restrict(
                    level.residue(level.c, PAD + 2 * j, 2 * c), level.d
                )

            rows_loop(0, rows // 2, 8, body)

        def up(level, rows, e_ref):
            def body(j, c):
                at = pl.ds(PAD + 2 * j, 2 * c)
                e = e_ref[pl.ds(PAD + j, c)]
                twice = jnp.stack([e, e], axis=1).reshape((2 * c, 8, 128))
                level.c[at] = level.c[at] + twice

            rows_loop(0, rows // 2, 8, body)
            level.sweep(PAD, PAD + rows, level.c, level.b)
            level.sweep(PAD, PAD + rows, level.b, level.c)

        down(L2, ny2, L3)
        down(L3, ny3, L4)
        L4.start(PAD, PAD + ny4, L4.b)
        L4.sweep(PAD, PAD + ny4, L4.b, L4.c)

        def twice_4(i, carry):
            L4.sweep(PAD, PAD + ny4, L4.c, L4.b)
            L4.sweep(PAD, PAD + ny4, L4.b, L4.c)
            return carry

        lax.fori_loop(0, (COARSE_SWEEPS - 2) // 2, twice_4, 0)
        up(L3, ny3, L4.c)
        up(L2, ny2, L3.c)

        first2 = PAD + me * (R // 4)
        for j in range(own1 - 3, end1 + 3):
            c1[j] = c1[j] + c2[first2 + (j - H1) // 2]
        L1.sweep(own1 - 2, end1 + 2, c1, b1)
        L1.sweep(own1 - 1, end1 + 1, b1, c1)

        def add_fine(j, c):
            at = pl.ds(2 * j, 2 * c)
            e = c1[pl.ds(j, c)]
            twice = jnp.stack([e, e], axis=1).reshape((2 * c, 8, 128))
            for k in range(2):
                c0[at, k] = c0[at, k] + twice

        rows_loop(own1 - 1, end1 + 1, 5, add_fine)
        sweep0(top - 1, bottom + 1, c0, g0, b0)
        if which == 1:
            sweep0(top, bottom, b0, g0, dst)

    vcycle(start_w, gather_1, 1, first_w)
    halo_start(first_w, 2)

    def store_f(s, y):
        f_ref[0, :, s * 256 : (s + 1) * 256] = y

    natural(first_w, top, R, 0, store_f)
    vcycle(first_w, gather_2, 2, c0)

    half = R // 2

    def to_next(h):
        return pltpu.make_async_remote_copy(
            src_ref=end_nat.at[pl.ds(h * half, half)],
            dst_ref=out_ref.at[0, pl.ds(h * half, half)],
            send_sem=end_send.at[h],
            recv_sem=end_recv.at[h],
            device_id={"tm": lax.rem(mine_t + 1, intervals)},
            device_id_type=MESH,
        )

    for h in range(2):
        sweep0(top + h * half, top + (h + 1) * half, b0, first_w, c0)

        def store_end(s, y, h=h):
            end_nat[h * half : (h + 1) * half, s * 256 : (s + 1) * 256] = y

        natural(c0, top + h * half, half, h * 8 * R, store_end)

        @pl.when(mine_t < intervals - 1)
        def _(h=h):
            to_next(h).start()

    @pl.when(mine_t == 0)
    def _():
        out_ref[...] = c_ref[...]

    halo_sent(cond0, 0)
    halo_sent(start_w, 1)
    halo_sent(first_w, 2)
    gather_sent(gather_cond, 0)
    gather_sent(gather_1, 1)
    gather_sent(gather_2, 2)

    @pl.when(mine_t > 0)
    def _():
        for h in range(2):
            to_next(h).wait_recv()

    @pl.when(mine_t < intervals - 1)
    def _():
        for h in range(2):
            to_next(h).wait_send()


def pack4(x):
    a, b = pair_rows(x)
    return jnp.where((iota(a.shape, 2) & 1) == 0, a, b)


def unpack4(ref, dst):
    x = ref[...]
    x = x.reshape((x.shape[0] * x.shape[1],) + x.shape[2:])
    even = (iota(x.shape, 2) & 1) == 0
    a = jnp.where(even, x, roll(x, 1, 2))
    b = jnp.where(even, roll(x, 127, 2), x)
    rows = x.shape[0]
    dst[pl.ds(PAD, 2 * rows)] = jnp.stack([a, b], axis=1).reshape((2 * rows,) + x.shape[1:])


def solution(mesh):
    n, intervals = mesh.shape["space"], mesh.shape["tm"]

    def per_device(ids, table, c_points):
        _, R, nx = c_points.shape
        ny = R * n
        window = R + 2 * HALO
        f32 = jnp.float32

        def tiles(*lead):
            return pltpu.VMEM(lead + (8, 128), f32)

        scratch = [pltpu.VMEM(ids.shape, ids.dtype), pltpu.VMEM(c_points.shape, f32)]
        scratch += [pltpu.VMEM((16 * R, 128), f32)]
        names = ["start_w", "first_w", "b0", "c0", "cond0", "fv0", "w0", "e0", "diag0", "om0"]
        for name in names:
            scratch.append(tiles(window) if name == "e0" else tiles(window, 2))
        scratch += [tiles(window // 2) for _ in range(9)]
        for level in (2, 3, 4):
            scratch += [tiles(ny // 2**level + 2 * PAD) for _ in range(9)]
        scratch += [tiles(n, R // 8) for _ in range(3)]
        scratch += [pltpu.VMEM((R, nx), f32)]
        scratch += [
            pltpu.SemaphoreType.DMA((6,)),
            pltpu.SemaphoreType.DMA((6,)),
            pltpu.SemaphoreType.DMA((3 * n,)),
            pltpu.SemaphoreType.DMA((3 * n,)),
            pltpu.SemaphoreType.DMA((2,)),
            pltpu.SemaphoreType.DMA((2,)),
            pltpu.SemaphoreType.DMA((2,)),
        ]
        hbm = pl.BlockSpec(memory_space=pltpu.HBM)
        vmem = pl.BlockSpec(memory_space=pltpu.VMEM)
        return pl.pallas_call(
            functools.partial(kernel, n, intervals, ny),
            out_shape=[jax.ShapeDtypeStruct(c_points.shape, f32)] * 2,
            in_specs=[hbm, pl.BlockSpec(memory_space=pltpu.SMEM), hbm],
            out_specs=[vmem, vmem],
            scratch_shapes=scratch,
            compiler_params=pltpu.CompilerParams(
                collective_id=0, has_side_effects=True, vmem_limit_bytes=40 * 1024 * 1024
            ),
        )(ids, table, c_points)

    return jax.shard_map(
        per_device,
        mesh=mesh,
        in_specs=(P("space", None), P(), P("tm", "space", None)),
        out_specs=(P("tm", "space", None), P("tm", "space", None)),
        check_vma=False,
    )
```

```python
import functools

import jax
import jax.numpy as jnp
from jax import lax
from jax.experimental import pallas as pl
from jax.experimental.pallas import tpu as pltpu
from jax.sharding import PartitionSpec as P

MESH = pl.DeviceIdType.MESH
MATS = 8
COARSE_SWEEPS = 16
DIFFUSION = 1024.0
HALO = 12
H1 = HALO // 2
PAD = 2


def rows_loop(lo, hi, size, body):
    count = hi - lo
    full = count // size
    if full == 1:
        body(lo, size)
    elif full > 1:

        def step(i, carry):
            body(lo + i * size, size)
            return carry

        lax.fori_loop(0, full, step, 0)
    if count % size:
        body(lo + full * size, count % size)


def iota(shape, dim):
    return lax.broadcasted_iota(jnp.int32, shape, dim)


def roll(x, by, axis):
    return pltpu.roll(x, by, axis)


def from_west(x, d):
    r = roll(x, d, 2)
    return jnp.where(iota(x.shape, 2) < d, roll(r, 1, 1), r)


def from_east(x, d):
    r = roll(x, 128 - d, 2)
    return jnp.where(iota(x.shape, 2) >= 128 - d, roll(r, 7, 1), r)


def first_col(shape, d):
    return (iota(shape, 1) == 0) & (iota(shape, 2) < d)


def last_col(shape, d):
    return (iota(shape, 1) == 7) & (iota(shape, 2) >= 128 - d)


def partner(x, d):
    return jnp.where((iota(x.shape, 2) & d) == 0, roll(x, 128 - d, 2), roll(x, d, 2))


def pair_rows(x):
    x = x.reshape((x.shape[0] // 2, 2) + x.shape[1:])
    return x[:, 0], x[:, 1]


def restrict(x, d):
    a, b = pair_rows(x)
    t = a + b
    return 0.25 * (t + partner(t, d))


def split3(x):
    hi = x.astype(jnp.bfloat16)
    rest = x - hi.astype(jnp.float32)
    mid = rest.astype(jnp.bfloat16)
    lo = (rest - mid.astype(jnp.float32)).astype(jnp.bfloat16)
    return hi, mid, lo


def dot(a, b):
    return jnp.dot(a, b, preferred_element_type=jnp.float32)


def compact(x):
    keep = (iota(x.shape, 2) & 7) == iota(x.shape, 1)
    return jnp.sum(jnp.where(keep, x, 0.0), axis=1)


def spread(x):
    shape = (x.shape[0], 8, 128)
    y = jnp.broadcast_to(x[:, None, :], shape)
    y = jnp.where((iota(shape, 2) & 7) == iota(shape, 1), y, 0.0)
    for d in (1, 2, 4):
        y = y + partner(y, d)
    return y


def coarsest(cond, scale):
    half, shape, rows = 0.5 * scale, cond.shape, cond.shape[0]
    row, lane = iota(shape, 0), iota(shape, 1)

    def west_of(v):
        return jnp.where(lane < 8, roll(v, 9, 1), roll(v, 8, 1))

    def east_of(v):
        return jnp.where(lane >= 120, roll(v, 119, 1), roll(v, 120, 1))

    def north_of(v):
        return roll(v, 1, 0)

    def south_of(v):
        return roll(v, rows - 1, 0)

    moves = (north_of, south_of, west_of, east_of)
    outside = (row == 0, row == rows - 1, lane == 0, lane == 127)
    faces, masked = [], []
    for move, out in zip(moves, outside):
        face = half * (cond + jnp.where(out, 0.0, move(cond)))
        faces.append(face)
        masked.append(jnp.where(out, 0.0, face))
    north, south, west, east = faces
    diag = 1.0 + ((north + south) + (west + east))
    om = 0.8 / diag
    return moves, [om * m for m in masked], om


class Level:
    def __init__(self, refs, d, scale, size):
        self.cond, self.fv, self.w, self.e, self.diag, self.om, self.g, self.b, self.c = refs
        self.d, self.scale, self.size = d, scale, size

    def setup(self, lo, hi, first_row, last_row, base):
        d, half = self.d, self.scale * 0.5

        def body(r, c):
            cond = self.cond
            here = cond[pl.ds(r, c)]
            shape = here.shape
            n = half * (here + cond[pl.ds(r - 1, c)])
            s = half * (here + cond[pl.ds(r + 1, c)])
            out_w, out_e = first_col(shape, d), last_col(shape, d)
            w = half * (here + jnp.where(out_w, 0.0, from_west(here, d)))
            e = half * (here + jnp.where(out_e, 0.0, from_east(here, d)))
            diag = 1.0 + ((n + s) + (w + e))
            row = iota(shape, 0) + (r + base)
            self.fv[pl.ds(r, c)] = jnp.where((row > first_row) & (row <= last_row), n, 0.0)
            self.w[pl.ds(r, c)] = jnp.where(out_w, 0.0, w)
            self.e[pl.ds(r, c)] = jnp.where(out_e, 0.0, e)
            self.diag[pl.ds(r, c)] = diag
            self.om[pl.ds(r, c)] = 0.8 / diag

        rows_loop(lo, hi, self.size, body)

    def beside(self, v, r, c):
        here = v[pl.ds(r, c)]
        nb = (
            self.fv[pl.ds(r, c)] * v[pl.ds(r - 1, c)]
            + self.fv[pl.ds(r + 1, c)] * v[pl.ds(r + 1, c)]
        ) + (
            self.w[pl.ds(r, c)] * from_west(here, self.d)
            + self.e[pl.ds(r, c)] * from_east(here, self.d)
        )
        return here, nb

    def start(self, lo, hi, dst):
        def body(r, c):
            dst[pl.ds(r, c)] = self.om[pl.ds(r, c)] * self.g[pl.ds(r, c)]

        rows_loop(lo, hi, self.size, body)

    def sweep(self, lo, hi, src, dst):
        def body(r, c):
            here, nb = self.beside(src, r, c)
            dst[pl.ds(r, c)] = 0.2 * here + self.om[pl.ds(r, c)] * (self.g[pl.ds(r, c)] + nb)

        rows_loop(lo, hi, self.size, body)

    def residue(self, v, r, c):
        here, nb = self.beside(v, r, c)
        return self.g[pl.ds(r, c)] - (self.diag[pl.ds(r, c)] * here - nb)


def kernel(
    n, intervals, ny,
    ids_hbm, table_ref, c_hbm, f_ref, out_ref,
    ids_ref, c_ref,
    turn, start_w, first_w, b0, c0, cond0, fv0, w0, e0, diag0, om0,
    cond1, fv1, w1, e1, diag1, om1, g1, b1, c1,
    cond2, fv2, w2, e2, diag2, om2, g2, b2, c2,
    cond3, fv3, w3, e3, diag3, om3, g3, b3, c3,
    g4, c4, om4, n4, s4, w4, e4,
    gather_cond, gather_1, gather_2, end_nat,
    halo_send, halo_recv, gat_send, gat_recv, end_send, end_recv, in_sem,
):
    load_ids = pltpu.make_async_copy(ids_hbm, ids_ref, in_sem.at[0])
    load_c = pltpu.make_async_copy(c_hbm, c_ref, in_sem.at[1])
    load_ids.start()
    load_c.start()
    me = lax.axis_index("space")
    mine_t = lax.axis_index("tm")
    R = c_ref.shape[1]
    top, bottom = HALO, HALO + R
    window = R + 2 * HALO

    barrier = pltpu.get_barrier_semaphore()
    for j in range(1, n):
        pl.semaphore_signal(barrier, 1, device_id={"space": lax.rem(me + j, n)}, device_id_type=MESH)

    for j in (1, intervals - 1):
        next_t = lax.rem(mine_t + j, intervals)
        pl.semaphore_signal(barrier, 1, device_id={"tm": next_t}, device_id_type=MESH)

    def halo_copies(ref, which):
        up = pltpu.make_async_remote_copy(
            src_ref=ref.at[pl.ds(top, HALO)],
            dst_ref=ref.at[pl.ds(bottom, HALO)],
            send_sem=halo_send.at[2 * which],
            recv_sem=halo_recv.at[2 * which],
            device_id={"space": lax.rem(me + n - 1, n)},
            device_id_type=MESH,
        )
        down = pltpu.make_async_remote_copy(
            src_ref=ref.at[pl.ds(bottom - HALO, HALO)],
            dst_ref=ref.at[pl.ds(0, HALO)],
            send_sem=halo_send.at[2 * which + 1],
            recv_sem=halo_recv.at[2 * which + 1],
            device_id={"space": lax.rem(me + 1, n)},
            device_id_type=MESH,
        )
        return up, down

    def halo_start(ref, which):
        up, down = halo_copies(ref, which)

        @pl.when(me > 0)
        def _():
            up.start()

        @pl.when(me < n - 1)
        def _():
            down.start()

    def halo_arrive(ref, which):
        up, down = halo_copies(ref, which)
        zero = jnp.zeros((HALO,) + ref.shape[1:], jnp.float32)

        @pl.when(me > 0)
        def _():
            down.wait_recv()

        @pl.when(me == 0)
        def _():
            ref[pl.ds(0, HALO)] = zero

        @pl.when(me < n - 1)
        def _():
            up.wait_recv()

        @pl.when(me == n - 1)
        def _():
            ref[pl.ds(bottom, HALO)] = zero

    def halo_sent(ref, which):
        up, down = halo_copies(ref, which)

        @pl.when(me > 0)
        def _():
            up.wait_send()

        @pl.when(me < n - 1)
        def _():
            down.wait_send()

    def gather_copy(ref, which, j, slot):
        return pltpu.make_async_remote_copy(
            src_ref=ref.at[slot],
            dst_ref=ref.at[slot],
            send_sem=gat_send.at[which * n + j],
            recv_sem=gat_recv.at[which * n + j],
            device_id={"space": lax.rem(me + j, n)},
            device_id_type=MESH,
        )

    def gather_start(ref, which):
        for j in range(1, n):
            gather_copy(ref, which, j, me).start()

    def gather_arrive(ref, which):
        for j in range(1, n):
            gather_copy(ref, which, j, lax.rem(me + n - j, n)).wait_recv()

    def gather_sent(ref, which):
        for j in range(1, n):
            gather_copy(ref, which, j, me).wait_send()

    row_i, col_i = iota((256, 256), 0), iota((256, 256), 1)
    into = jnp.where(col_i == (row_i & 1) * 128 + (row_i >> 1), 1.0, 0.0).astype(jnp.bfloat16)

    def put_turned(y):
        for k in range(2):
            turn[pl.ds(k * 8 * R, 8 * R), :] = y[:, k * 128 : (k + 1) * 128]

    def chunks(x):
        return jnp.concatenate([x[:, s * 256 : (s + 1) * 256] for s in range(8)], axis=0)

    load_ids.wait()
    put_turned(dot(chunks(ids_ref[...].astype(jnp.float32)).astype(jnp.bfloat16), into))
    for r in range(R):
        for k in range(2):
            kind = turn[pl.ds(k * 8 * R + r, 8, stride=R), :]
            value = jnp.zeros((8, 128), jnp.float32)
            for m in range(MATS):
                value = jnp.where(kind == float(m), table_ref[m], value)
            cond0[top + r, k] = value

    def natural(src, row0, rows, base, store):
        for r in range(rows):
            for k in range(2):
                turn[pl.ds(base + k * 8 * rows + r, 8, stride=rows), :] = src[row0 + r, k]
        back = jnp.where(row_i == (col_i & 1) * 128 + (col_i >> 1), 1.0, 0.0).astype(jnp.bfloat16)
        x = jnp.concatenate(
            [turn[pl.ds(base, 8 * rows), :], turn[pl.ds(base + 8 * rows, 8 * rows), :]], axis=1
        )
        y = sum(dot(part, back) for part in split3(x))
        for s in range(8):
            store(s, y[s * rows : (s + 1) * rows])

    pl.semaphore_wait(barrier, n + 1)

    halo_start(cond0, 0)
    load_c.wait()
    put_turned(sum(dot(part, into) for part in split3(chunks(c_ref[0]))))
    for r in range(R):
        for k in range(2):
            start_w[top + r, k] = turn[pl.ds(k * 8 * R + r, 8, stride=R), :]
    halo_start(start_w, 1)

    scale = DIFFUSION
    L1 = Level((cond1, fv1, w1, e1, diag1, om1, g1, b1, c1), 1, scale / 4, 16)
    L2 = Level((cond2, fv2, w2, e2, diag2, om2, g2, b2, c2), 2, scale / 16, 32)
    L3 = Level((cond3, fv3, w3, e3, diag3, om3, g3, b3, c3), 4, scale / 64, 16)
    ny2, ny3, ny4 = ny // 4, ny // 8, ny // 16

    def coarsen_cond(lo, hi):
        def body(j, c):
            x = cond0[pl.ds(2 * j, 2 * c)]
            a, b = pair_rows(x)
            t = a + b
            cond1[pl.ds(j, c)] = 0.25 * (t[:, 0] + t[:, 1])

        rows_loop(lo, hi, 4, body)

    coarsen_cond(H1, H1 + R // 2)
    gather_cond[me] = pack4(restrict(cond1[pl.ds(H1, R // 2)], 1))
    gather_start(gather_cond, 0)

    zero_pad = jnp.zeros((PAD, 8, 128), jnp.float32)
    for level, rows in ((L2, ny2), (L3, ny3)):
        for ref in (level.cond, level.b, level.c, level.fv):
            ref[pl.ds(0, PAD)] = zero_pad
            ref[pl.ds(PAD + rows, PAD)] = zero_pad

    halo_arrive(cond0, 0)
    coarsen_cond(0, H1)
    coarsen_cond(H1 + R // 2, R // 2 + 2 * H1)
    base0 = me * R - HALO
    half0 = scale * 0.5

    def setup0(r, c):
        here0, here1 = cond0[pl.ds(r, c), 0], cond0[pl.ds(r, c), 1]
        shape = here0.shape
        out_w, out_e = first_col(shape, 1), last_col(shape, 1)
        mid = half0 * (here0 + here1)
        west = half0 * (here0 + jnp.where(out_w, 0.0, from_west(here1, 1)))
        east = half0 * (here1 + jnp.where(out_e, 0.0, from_east(here0, 1)))
        row = iota(shape, 0) + (r + base0)
        inside = (row > 0) & (row <= ny - 1)
        for k, here, we in ((0, here0, west + mid), (1, here1, mid + east)):
            north = half0 * (here + cond0[pl.ds(r - 1, c), k])
            south = half0 * (here + cond0[pl.ds(r + 1, c), k])
            diag = 1.0 + ((north + south) + we)
            fv0[pl.ds(r, c), k] = jnp.where(inside, north, 0.0)
            diag0[pl.ds(r, c), k] = diag
            om0[pl.ds(r, c), k] = 0.8 / diag
        w0[pl.ds(r, c), 0] = jnp.where(out_w, 0.0, west)
        w0[pl.ds(r, c), 1] = mid
        e0[pl.ds(r, c)] = jnp.where(out_e, 0.0, east)

    rows_loop(1, window - 1, 10, setup0)
    L1.setup(1, R // 2 + 2 * H1 - 1, 0, ny // 2 - 1, me * (R // 2) - H1)

    def setup_low():
        gather_arrive(gather_cond, 0)
        unpack4(gather_cond, cond2)
        cond3[pl.ds(PAD, ny3)] = restrict(cond2[pl.ds(PAD, ny2)], 2)
        _, sides, om = coarsest(compact(restrict(cond3[pl.ds(PAD, ny3)], 4)), scale / 256)
        om4[...] = om
        for ref, side in zip((n4, s4, w4, e4), sides):
            ref[...] = side
        for level, rows in ((L2, ny2), (L3, ny3)):
            level.setup(PAD, PAD + rows, 0, rows - 1, -PAD)

    def beside0(v, r, c):
        v0, v1 = v[pl.ds(r, c), 0], v[pl.ds(r, c), 1]
        up, down = pl.ds(r - 1, c), pl.ds(r + 1, c)
        at = pl.ds(r, c)
        mid = w0[at, 1]
        nb0 = (fv0[at, 0] * v[up, 0] + fv0[down, 0] * v[down, 0]) + (
            w0[at, 0] * from_west(v1, 1) + mid * v1
        )
        nb1 = (fv0[at, 1] * v[up, 1] + fv0[down, 1] * v[down, 1]) + (
            mid * v0 + e0[at] * from_east(v0, 1)
        )
        return (v0, v1), (nb0, nb1)

    def sweep0(lo, hi, src, g, dst):
        def body(r, c):
            here, nb = beside0(src, r, c)
            at = pl.ds(r, c)
            for k in range(2):
                dst[at, k] = 0.2 * here[k] + om0[at, k] * (g[at, k] + nb[k])

        rows_loop(lo, hi, {14: 14, 8: 8, 16: 16, 18: 9}.get(hi - lo, 12), body)

    def vcycle(g0, gathered, which, dst):
        sweep0(top + 1, bottom - 1, g0, g0, b0)
        sweep0(top + 2, bottom - 2, b0, g0, c0)
        halo_arrive(g0, which)
        sweep0(top - 10, top + 1, g0, g0, b0)
        sweep0(bottom - 1, bottom + 10, g0, g0, b0)
        sweep0(top - 9, top + 2, b0, g0, c0)
        sweep0(bottom - 2, bottom + 9, b0, g0, c0)

        def to_level_1(j, c):
            r, rows = 2 * j, 2 * c
            here, nb = beside0(c0, r, rows)
            at = pl.ds(r, rows)
            r0 = g0[at, 0] - (diag0[at, 0] * here[0] - nb[0])
            r1 = g0[at, 1] - (diag0[at, 1] * here[1] - nb[1])
            a, b = pair_rows(r0 + r1)
            g1[pl.ds(j, c)] = 0.25 * (a + b)

        own1, end1 = H1, H1 + R // 2
        rows_loop(own1 - 4, end1 + 4, 8, to_level_1)
        L1.start(own1 - 4, end1 + 4, b1)
        L1.sweep(own1 - 3, end1 + 3, b1, c1)
        gathered[me] = pack4(restrict(L1.residue(c1, own1, R // 2), 1))
        gather_start(gathered, which)
        if which == 1:
            setup_low()
        gather_arrive(gathered, which)
        unpack4(gathered, g2)

        def down(level, rows, coarse_g):
            level.start(PAD, PAD + rows, level.b)
            level.sweep(PAD, PAD + rows, level.b, level.c)

            def body(j, c):
                coarse_g[pl.ds(PAD + j, c)] = restrict(
                    level.residue(level.c, PAD + 2 * j, 2 * c), level.d
                )

            rows_loop(0, rows // 2, 16, body)

        def up(level, rows, e_ref):
            def body(j, c):
                at = pl.ds(PAD + 2 * j, 2 * c)
                e = e_ref[pl.ds(PAD + j, c)]
                twice = jnp.stack([e, e], axis=1).reshape((2 * c, 8, 128))
                level.c[at] = level.c[at] + twice

            rows_loop(0, rows // 2, 16, body)
            level.sweep(PAD, PAD + rows, level.c, level.b)
            level.sweep(PAD, PAD + rows, level.b, level.c)

        down(L2, ny2, g3)
        down(L3, ny3, g4)
        lane = iota((ny4, 128), 1)
        first = om4[...] * compact(g4[pl.ds(PAD, ny4)])

        def sweep4(i, v):
            west = jnp.where(lane < 8, roll(v, 9, 1), roll(v, 8, 1))
            east = jnp.where(lane >= 120, roll(v, 119, 1), roll(v, 120, 1))
            nb = (n4[...] * roll(v, 1, 0) + s4[...] * roll(v, ny4 - 1, 0)) + (
                w4[...] * west + e4[...] * east
            )
            return (0.2 * v + first) + nb

        c4[pl.ds(PAD, ny4)] = spread(lax.fori_loop(0, COARSE_SWEEPS - 1, sweep4, first, unroll=5))
        up(L3, ny3, c4)
        up(L2, ny2, L3.c)

        first2 = PAD + me * (R // 4)
        for j in range(own1 - 3, end1 + 3):
            c1[j] = c1[j] + c2[first2 + (j - H1) // 2]
        L1.sweep(own1 - 2, end1 + 2, c1, b1)
        L1.sweep(own1 - 1, end1 + 1, b1, c1)

        def add_fine(j, c):
            at = pl.ds(2 * j, 2 * c)
            e = c1[pl.ds(j, c)]
            twice = jnp.stack([e, e], axis=1).reshape((2 * c, 8, 128))
            for k in range(2):
                c0[at, k] = c0[at, k] + twice

        rows_loop(own1 - 1, end1 + 1, 10, add_fine)
        sweep0(top - 1, bottom + 1, c0, g0, b0)
        if which == 1:
            sweep0(top, bottom, b0, g0, dst)

    vcycle(start_w, gather_1, 1, first_w)
    halo_start(first_w, 2)

    def store_f(s, y):
        f_ref[0, :, s * 256 : (s + 1) * 256] = y

    natural(first_w, top, R, 0, store_f)
    vcycle(first_w, gather_2, 2, c0)

    half = R // 2

    def to_next(h):
        return pltpu.make_async_remote_copy(
            src_ref=end_nat.at[pl.ds(h * half, half)],
            dst_ref=out_ref.at[0, pl.ds(h * half, half)],
            send_sem=end_send.at[h],
            recv_sem=end_recv.at[h],
            device_id={"tm": lax.rem(mine_t + 1, intervals)},
            device_id_type=MESH,
        )

    for h in range(2):
        sweep0(top + h * half, top + (h + 1) * half, b0, first_w, c0)

        def store_end(s, y, h=h):
            end_nat[h * half : (h + 1) * half, s * 256 : (s + 1) * 256] = y

        natural(c0, top + h * half, half, h * 8 * R, store_end)

        @pl.when(mine_t < intervals - 1)
        def _(h=h):
            to_next(h).start()

    @pl.when(mine_t == 0)
    def _():
        out_ref[...] = c_ref[...]

    halo_sent(cond0, 0)
    halo_sent(start_w, 1)
    halo_sent(first_w, 2)
    gather_sent(gather_cond, 0)
    gather_sent(gather_1, 1)
    gather_sent(gather_2, 2)

    @pl.when(mine_t > 0)
    def _():
        for h in range(2):
            to_next(h).wait_recv()

    @pl.when(mine_t < intervals - 1)
    def _():
        for h in range(2):
            to_next(h).wait_send()


def pack4(x):
    a, b = pair_rows(x)
    return jnp.where((iota(a.shape, 2) & 1) == 0, a, b)


def unpack4(ref, dst):
    x = ref[...]
    x = x.reshape((x.shape[0] * x.shape[1],) + x.shape[2:])
    even = (iota(x.shape, 2) & 1) == 0
    a = jnp.where(even, x, roll(x, 1, 2))
    b = jnp.where(even, roll(x, 127, 2), x)
    rows = x.shape[0]
    dst[pl.ds(PAD, 2 * rows)] = jnp.stack([a, b], axis=1).reshape((2 * rows,) + x.shape[1:])


def solution(mesh):
    n, intervals = mesh.shape["space"], mesh.shape["tm"]

    def per_device(ids, table, c_points):
        _, R, nx = c_points.shape
        ny = R * n
        window = R + 2 * HALO
        f32 = jnp.float32

        def tiles(*lead):
            return pltpu.VMEM(lead + (8, 128), f32)

        scratch = [pltpu.VMEM(ids.shape, ids.dtype), pltpu.VMEM(c_points.shape, f32)]
        scratch += [pltpu.VMEM((16 * R, 128), f32)]
        names = ["start_w", "first_w", "b0", "c0", "cond0", "fv0", "w0", "e0", "diag0", "om0"]
        for name in names:
            scratch.append(tiles(window) if name == "e0" else tiles(window, 2))
        scratch += [tiles(window // 2) for _ in range(9)]
        for level in (2, 3):
            scratch += [tiles(ny // 2**level + 2 * PAD) for _ in range(9)]
        scratch += [tiles(ny // 16 + 2 * PAD) for _ in range(2)]
        scratch += [pltpu.VMEM((ny // 16, 128), f32) for _ in range(5)]
        scratch += [tiles(n, R // 8) for _ in range(3)]
        scratch += [pltpu.VMEM((R, nx), f32)]
        scratch += [
            pltpu.SemaphoreType.DMA((6,)),
            pltpu.SemaphoreType.DMA((6,)),
            pltpu.SemaphoreType.DMA((3 * n,)),
            pltpu.SemaphoreType.DMA((3 * n,)),
            pltpu.SemaphoreType.DMA((2,)),
            pltpu.SemaphoreType.DMA((2,)),
            pltpu.SemaphoreType.DMA((2,)),
        ]
        hbm = pl.BlockSpec(memory_space=pltpu.HBM)
        vmem = pl.BlockSpec(memory_space=pltpu.VMEM)
        return pl.pallas_call(
            functools.partial(kernel, n, intervals, ny),
            out_shape=[jax.ShapeDtypeStruct(c_points.shape, f32)] * 2,
            in_specs=[hbm, pl.BlockSpec(memory_space=pltpu.SMEM), hbm],
            out_specs=[vmem, vmem],
            scratch_shapes=scratch,
            compiler_params=pltpu.CompilerParams(
                collective_id=0, has_side_effects=True, vmem_limit_bytes=40 * 1024 * 1024
            ),
        )(ids, table, c_points)

    return jax.shard_map(
        per_device,
        mesh=mesh,
        in_specs=(P("space", None), P(), P("tm", "space", None)),
        out_specs=(P("tm", "space", None), P("tm", "space", None)),
        check_vma=False,
    )
```
